256 devices in a mesh: bend: 2 (over core), head: 8 (over z), blk: 16 (over y, x).
Axes of the slice: x: 4, y: 4, z: 8, core: 2. Of those that a mesh axis runs over, the one named last changes fastest.
Arguments:
- queries: bfloat16 [32768, 1024], P(('bend', 'head', 'blk')), parts along dimension 0, may hold values from -6 to 6
- keys_in: bfloat16 [32768, 1024], P(('bend', 'head', 'blk')), parts along dimension 0, may hold values from -6 to 6
- values: bfloat16 [32768, 1024], P(('bend', 'head', 'blk')), parts along dimension 0, may hold values from -6 to 6
- d_out: bfloat16 [32768, 1024], P(('bend', 'head', 'blk')), parts along dimension 0, may hold values from -6 to 6
- token_count: int32 [2], P('bend'), parts along dimension 0, may hold values from 8192 to 16384
- block_ids: int32 [256], P('bend'), parts along dimension 0, may hold values from 0 to 127, each once
- neighbours: int32 [256, 10], P('bend'), parts along dimension 0, may hold values from 0 to 127, as said below
Outputs:
- grad_queries: bfloat16 [32768, 1024], P(('bend', 'head', 'blk')), parts along dimension 0
- grad_keys: bfloat16 [32768, 1024], P(('bend', 'head', 'blk')), parts along dimension 0
- grad_values: bfloat16 [32768, 1024], P(('bend', 'head', 'blk')), parts along dimension 0
The draws below stay inside these ranges and needn't reach their ends.
There are 2 independent parts, one for each index of `bend`. The reference program is written for one: setup_inputs(seed, part) draws one part's arguments, and reference() takes and returns one part's arrays. A program takes and returns all parts, laid end to end along the dimension named above; each array names one. Nothing has to cross between parts.
Inputs may be any that keep to these rules, and one draw needn't show every extreme that they name: `neighbours`: column 0 of a row is the query block itself; the 10 entries of a row are distinct; every block appears in exactly 10 rows.
All inputs are finite; a program needn't handle non-finite values.
Results may differ from the reference program's by a relative error of at most 0.017.
Values may be sent and summed in bfloat16 or wider, within the bound.
No kernel may reach another device: no remote copies, remote signals or barrier semaphores. Data moves between devices by JAX's collectives and lax.ppermute only.
A program may use at most 128 MiB of HBM per device.

```python
import math
import jax
import jax.numpy as jnp
from jax import lax

H = 16
HD = 64
D = 1024
BLK = 128
NBR = 10
TOKENS = 16384
NBLK = 128


def draw_queries(key, part):
    sample = jnp.clip(jax.random.normal(jax.random.fold_in(key, 11), (TOKENS, D), jnp.float32), -6.0, 6.0)
    return sample.astype(jnp.bfloat16)


def draw_keys_in(key, part):
    sample = jnp.clip(jax.random.normal(jax.random.fold_in(key, 12), (TOKENS, D), jnp.float32), -6.0, 6.0)
    return sample.astype(jnp.bfloat16)


def draw_neighbours(key, part):
    count_blocks = TOKENS // BLK
    row_ids = jnp.arange(count_blocks, dtype=jnp.int32)
    relabel = jax.random.permutation(jax.random.fold_in(key, 31), count_blocks).astype(jnp.int32)
    inverse = jnp.argsort(relabel, stable=True).astype(jnp.int32)
    shifts = (1 + jax.random.permutation(jax.random.fold_in(key, 32), count_blocks - 1)[:NBR - 1]).astype(jnp.int32)
    moved = (relabel[:, None] + shifts[None, :]) % count_blocks
    others = inverse[moved].astype(jnp.int32)
    return jnp.concatenate([row_ids[:, None], others], axis=1).astype(jnp.int32)


def steps_of(stream_key, extent, cuts, low, high):
    level, own = 1.0, jax.random.fold_in(stream_key, 6)
    for dim, parts in cuts:
        draws = jnp.exp(jax.random.uniform(jax.random.fold_in(own, dim), (parts,), jnp.float32, low / len(cuts), high / len(cuts)))
        level = level * jnp.repeat(draws, extent[dim] // parts).reshape([-1 if axis == dim else 1 for axis in range(len(extent))])
    return level


def bell_draw(stream_key, shape, width, limit, cuts=(), held_as=jnp.bfloat16):
    result = jax.random.normal(stream_key, shape, jnp.float32) * width
    if len(cuts) > 0:
        result = steps_of(stream_key, shape, cuts, -0.22, 0.18) * result
    return jnp.clip(result, min=-limit, max=limit).astype(held_as)


def setup_inputs(seed: int = 0, part: int = 0) -> dict:
    keys = jax.random.split(jax.random.key(seed), 8)
    part_keys = jax.random.split(jax.random.fold_in(keys[7], part), 8)
    queries = draw_queries(jax.random.fold_in(jax.random.fold_in(keys[7], part), 71), part)
    keys_in = draw_keys_in(jax.random.fold_in(jax.random.fold_in(keys[7], part), 71), part)
    values = bell_draw(part_keys[2], (TOKENS, D), 1.0, 6.0, ((0, 128),))
    d_out = bell_draw(part_keys[3], (TOKENS, D), 1.0, 6.0, ((0, 128),))
    token_count = jax.random.randint(part_keys[4], (1,), TOKENS // 2, TOKENS + 1).astype(jnp.int32)
    block_ids = jax.random.permutation(part_keys[5], NBLK).astype(jnp.int32)
    neighbours = draw_neighbours(jax.random.fold_in(jax.random.fold_in(keys[7], part), 71), part)
    return {"queries": queries, "keys_in": keys_in, "values": values, "d_out": d_out, "token_count": token_count, "block_ids": block_ids, "neighbours": neighbours}


neg_fill = -1e+30

def reference(queries, keys_in, values, d_out, token_count, block_ids, neighbours):
    count_blocks = TOKENS // BLK
    score_scale = 1.0 / math.sqrt(HD)
    highest = lax.Precision.HIGHEST
    table_ids = jnp.arange(count_blocks, dtype=jnp.int32)
    matches = block_ids[None, :] == table_ids[:, None]
    stored_of = lax.optimization_barrier(jnp.sum(jnp.where(matches, table_ids[None, :], 0), axis=1)).astype(jnp.int32)
    token_limit = token_count[0]
    offsets = jnp.arange(BLK, dtype=jnp.int32)
    row_where = (block_ids[:, None] * BLK + offsets[None, :]).reshape(-1)
    grad_rows = jnp.where((row_where < token_limit)[:, None], d_out, jnp.zeros_like(d_out))
    query_blocks = queries.reshape(count_blocks, BLK, H, HD)
    key_blocks = keys_in.reshape(count_blocks, BLK, H, HD)
    value_blocks = values.reshape(count_blocks, BLK, H, HD)
    grad_blocks = grad_rows.reshape(count_blocks, BLK, H, HD)
    zero_acc = jnp.zeros((count_blocks, BLK, H, HD), jnp.float32)

    def visit_block(running, stored):
        key_sum, value_sum = running
        global_id = block_ids[stored]
        near_global = neighbours[global_id].astype(jnp.int32)
        near_stored = stored_of[near_global].astype(jnp.int32)
        query_where = global_id * BLK + offsets
        key_where = near_global[:, None] * BLK + offsets[None, :]
        allowed = (key_where < token_limit)[None] | (key_where[None] == query_where[:, None, None])
        permit = allowed[None]
        query_tile = query_blocks[stored].astype(jnp.float32)
        grad_tile = grad_blocks[stored].astype(jnp.float32)
        key_tile = key_blocks[near_stored].astype(jnp.float32)
        value_tile = value_blocks[near_stored].astype(jnp.float32)
        product = jnp.einsum('qhd,jkhd->hqjk', query_tile, key_tile, precision=highest) * score_scale
        largest = lax.optimization_barrier(jnp.max(jnp.where(permit, product, neg_fill), axis=(2, 3), keepdims=True))
        denominator = lax.optimization_barrier(jnp.sum(jnp.where(permit, jnp.exp(product - largest), 0.0), axis=(2, 3), keepdims=True))
        log_total = largest + jnp.log(denominator)
        probability = jnp.where(permit, jnp.exp(product - log_total), 0.0)
        grad_probs = jnp.einsum('qhd,jkhd->hqjk', grad_tile, value_tile, precision=highest)
        row_delta = lax.optimization_barrier(jnp.sum(probability * grad_probs, axis=(2, 3), keepdims=True))
        prob_low = probability.astype(jnp.bfloat16)
        grad_scores = (probability * (grad_probs - row_delta)).astype(jnp.bfloat16)
        grad_wide = grad_scores.astype(jnp.float32)
        query_grad = (jnp.einsum('hqjk,jkhd->qhd', grad_wide, key_tile, precision=highest) * score_scale).astype(jnp.bfloat16)
        key_part = jnp.einsum('hqjk,qhd->jkhd', grad_wide, query_tile, precision=highest) * score_scale
        value_part = jnp.einsum('hqjk,qhd->jkhd', prob_low.astype(jnp.float32), grad_tile, precision=highest)
        key_sum = key_sum.at[near_stored].add(key_part)
        value_sum = value_sum.at[near_stored].add(value_part)
        return ((key_sum, value_sum), query_grad)
    (key_sum, value_sum), query_grads = lax.scan(visit_block, (zero_acc, zero_acc), table_ids)
    return (query_grads.reshape(TOKENS, D), key_sum.reshape(TOKENS, D).astype(jnp.bfloat16), value_sum.reshape(TOKENS, D).astype(jnp.bfloat16))
```

```python
import functools
import math

import jax
import jax.numpy as jnp
from jax import lax
from jax.experimental import pallas as pl
from jax.experimental.pallas import tpu as pltpu
from jax.sharding import Mesh, PartitionSpec as P

HD = 64
BLK = 128
HALF = 64
NBR = 10
HEADS = 16
NSRC = 32
NX = 4
SCALE = 1.0 / math.sqrt(HD)
C2 = SCALE * math.log2(math.e)
NEG = -1e30
BF = jnp.bfloat16
F32 = jnp.float32
NT = (((1,), (1,)), ((), ()))
NN = (((1,), (0,)), ((), ()))
VMEM = pl.BlockSpec(memory_space=pltpu.VMEM)
SMEM = pl.BlockSpec(memory_space=pltpu.SMEM)
ANY = pl.BlockSpec(memory_space=pl.ANY)
PARAMS = pltpu.CompilerParams(vmem_limit_bytes=40 * 2**20)


def cost(flops, nbytes):
    return pl.CostEstimate(flops=flops, bytes_accessed=nbytes, transcendentals=0)


def tables_kernel(row_ref, col_ref, nbr_ref, nbrt_ref, out_ref):
    n = 128
    sub = lax.broadcasted_iota(jnp.int32, (n, n), 0)
    lane = lax.broadcasted_iota(jnp.int32, (n, n), 1)
    b_of = (col_ref[:, 0:1] == lane).astype(F32).astype(BF)
    adj = jnp.zeros((n, n), F32)
    adj_t = jnp.zeros((n, n), F32)
    for k in range(NBR):
        adj = adj + (nbr_ref[:, k : k + 1] == lane).astype(F32)
        adj_t = adj_t + (nbrt_ref[k : k + 1, :] == sub).astype(F32)
    eye = (sub == lane).astype(F32)
    tri = (lane <= sub).astype(F32).astype(BF)

    def stored(a):
        right = lax.dot_general(a.astype(BF), b_of, NT, preferred_element_type=F32)
        return lax.dot_general(b_of, right.astype(BF), NN, preferred_element_type=F32) - eye

    out_ref[...] = jnp.zeros_like(out_ref)
    own = lax.broadcasted_iota(jnp.int32, (1, n), 1)
    for base, a in ((0, adj_t), (16, adj)):
        m = stored(a)
        rank = lax.dot_general(tri, m.astype(BF), NN, preferred_element_type=F32)
        out_ref[base : base + 1, :] = own
        for k in range(1, NBR):
            hit = jnp.where((rank == float(k)) & (m > 0.5), sub, 0)
            out_ref[base + k : base + k + 1, :] = jnp.sum(hit, axis=0, keepdims=True)
    out_ref[32:33, :] = row_ref[1:2, :] - row_ref[0:1, :] * BLK


def make_tables(block_ids, neighbours, token_count):
    row = jnp.concatenate(
        [block_ids[None, :], jnp.broadcast_to(token_count[:1, None], (1, 128)), jnp.zeros((6, 128), jnp.int32)], 0
    )
    nbrt = jnp.concatenate([neighbours.T, jnp.full((6, 128), -1, jnp.int32)], 0)
    return pl.pallas_call(
        tables_kernel,
        out_shape=jax.ShapeDtypeStruct((40, 128), jnp.int32),
        in_specs=[VMEM] * 4,
        out_specs=VMEM,
        compiler_params=PARAMS,
        name="tables",
    )(row, block_ids[:, None], neighbours, nbrt)


def pack_rows(out, base, a_ref, b_ref, row0, limit):
    rows = pl.ds(row0, HALF)
    keep = None
    if limit is not None:
        keep = (lax.broadcasted_iota(jnp.int32, (HALF, 128), 0) + row0) < limit
    for p in range(HEADS // 2):
        a = a_ref[rows, p * 128 : p * 128 + 128]
        b = b_ref[rows, p * 128 : p * 128 + 128]
        if keep is not None:
            b = jnp.where(keep, b.astype(F32), 0.0).astype(BF)
        out[base + 2 * p] = jnp.concatenate([a[:, :HD], b[:, :HD]], axis=1)
        out[base + 2 * p + 1] = jnp.concatenate([a[:, HD:], b[:, HD:]], axis=1)


def pack_other_kernel(meta, q_ref, k_ref, v_ref, g_ref, out_ref):
    row0 = pl.multiple_of((1 - meta[0]) * HALF, HALF)
    pack_rows(out_ref, 0, k_ref, v_ref, row0, None)
    pack_rows(out_ref, HEADS, q_ref, g_ref, row0, meta[1])


def pack_mine_kernel(meta, q_ref, k_ref, v_ref, g_ref, kv_ref, qg_ref):
    c = meta[0]
    row0 = pl.multiple_of(c * HALF, HALF)
    pack_rows(kv_ref, c * HEADS, k_ref, v_ref, row0, None)
    pack_rows(qg_ref, c * HEADS, q_ref, g_ref, row0, meta[1])


def unpack_kv_kernel(meta, full_ref, other_ref, k_ref, v_ref):
    c = meta[0]
    for src, base, half in ((full_ref, c * HEADS, c), (other_ref, 0, 1 - c)):
        rows = pl.ds(pl.multiple_of(half * HALF, HALF), HALF)
        for p in range(HEADS // 2):
            a = src[base + 2 * p]
            b = src[base + 2 * p + 1]
            k_ref[rows, p * 128 : p * 128 + 128] = jnp.concatenate([a[:, :HD], b[:, :HD]], axis=1)
            v_ref[rows, p * 128 : p * 128 + 128] = jnp.concatenate([a[:, HD:], b[:, HD:]], axis=1)


def unpack_q_kernel(meta, full_ref, other_ref, q_ref):
    c = meta[0]
    h2 = HALF // 2
    for src, base, half in ((full_ref, c * HEADS, c), (other_ref, 0, 1 - c)):
        lo = pl.ds(pl.multiple_of(half * HALF, HALF), h2)
        hi = pl.ds(pl.multiple_of(half * HALF + h2, h2), h2)
        for p in range(HEADS // 2):
            a = src[base + 2 * p]
            b = src[base + 2 * p + 1]
            q_ref[lo, p * 128 : p * 128 + 128] = jnp.concatenate([a[:, :HD], b[:, :HD]], axis=1)
            q_ref[hi, p * 128 : p * 128 + 128] = jnp.concatenate([a[:, HD:], b[:, HD:]], axis=1)


def fetch(pieces, dst, sems, c, x):
    half = NSRC // 2
    left, right, far = lax.rem(x + 3, NX), lax.rem(x + 1, NX), lax.rem(x + 2, NX)
    copies = []
    for side in range(2):
        o = c if side == 0 else 1 - c
        own, r1, l1, r2, l2 = pieces[5 * side : 5 * side + 5]
        for src, to in (
            (own, dst.at[o, x]),
            (r1, dst.at[o, left]),
            (l1, dst.at[o, right]),
            (r2, dst.at[o, far, pl.ds(0, half)]),
            (l2, dst.at[o, far, pl.ds(half, half)]),
        ):
            copies.append(pltpu.make_async_copy(src, to, sems.at[len(copies)]))
    return copies


def split_rows(tile):
    lane = lax.broadcasted_iota(jnp.int32, tile.shape, 1)
    wide = tile.astype(F32)
    top = jnp.where(lane < HD, wide, 0.0).astype(BF)
    bottom = jnp.where(lane >= HD, wide, 0.0).astype(BF)
    return jnp.concatenate([top, bottom], axis=0)


def query_kernel(meta, tab, qg_ref, *refs):
    pieces, (dq_ref, stat_ref, held, tiles, scores, sems) = refs[:10], refs[10:]
    c, x = meta[0], meta[2]
    copies = fetch(pieces, held, sems, c, x)
    for copy in copies:
        copy.start()
    for copy in copies:
        copy.wait()
    lane = lax.broadcasted_iota(jnp.int32, (HALF, 128), 1)
    sub = lax.broadcasted_iota(jnp.int32, (HALF, 128), 0)
    mine = lane == sub + c * HALF

    def step(s, carry):
        t = s * NX + x
        limits = []
        for k in range(NBR):
            u = tab[k, t]
            ux, us = lax.rem(u, NX), lax.div(u, NX)
            tiles[k * BLK : k * BLK + HALF] = held[0, ux, us]
            tiles[k * BLK + HALF : (k + 1) * BLK] = held[1, ux, us]
            limits.append(tab[32, u])
        lhs = split_rows(qg_ref[s])
        top = jnp.full((HALF, 128), NEG, F32)
        for j in range(NBR // 2):
            both = lax.dot_general(lhs, tiles[j * 256 : j * 256 + 256], NT, preferred_element_type=F32)
            for i in range(2):
                k = 2 * j + i
                ok = lane < limits[k]
                if k == 0:
                    ok = ok | mine
                sc = jnp.where(ok, both[:HALF, i * 128 : i * 128 + 128], NEG)
                scores[0, k] = sc
                scores[1, k] = both[HALF:, i * 128 : i * 128 + 128]
                top = jnp.maximum(top, sc)
        top = jnp.max(top, axis=1, keepdims=True) * C2
        total = jnp.zeros((HALF, 128), F32)
        dot = jnp.zeros((HALF, 128), F32)
        for k in range(NBR):
            p = jnp.exp2(scores[0, k] * C2 - top)
            scores[0, k] = p
            total = total + p
            dot = dot + p * scores[1, k]
        total = jnp.sum(total, axis=1, keepdims=True)
        delta = jnp.sum(dot, axis=1, keepdims=True) / total
        acc = jnp.zeros((HALF, 128), F32)
        for j in range(NBR // 2):
            ds = jnp.concatenate(
                [(scores[0, k] * (scores[1, k] - delta)).astype(BF) for k in (2 * j, 2 * j + 1)], axis=1
            )
            acc = acc + lax.dot_general(ds, tiles[j * 256 : j * 256 + 256], NN, preferred_element_type=F32)
        dq = (acc * (SCALE / total)).astype(BF)
        dq_ref[s] = jnp.concatenate([dq[: HALF // 2, :HD], dq[HALF // 2 :, :HD]], axis=1)
        lse = top + jnp.log2(total)
        stat = jnp.where(lane == sub, lse, 0.0) + jnp.where(lane == sub + HALF, delta, 0.0)
        stat_ref[pl.ds(s, 1), :] = jnp.sum(stat, axis=0, keepdims=True)
        return carry

    lax.fori_loop(0, NSRC, step, 0)


def key_kernel(meta, tab, kv_ref, stats_ref, *refs):
    pieces, (dkv_ref, held, tiles, lses, deltas, sems) = refs[:10], refs[10:]
    c, x = meta[0], meta[2]
    copies = fetch(pieces, held, sems, c, x)
    for copy in copies:
        copy.start()
    lane_n = lax.broadcasted_iota(jnp.int32, (NSRC, 128), 1)
    for i in range(NX):
        a, b = stats_ref[0, i], stats_ref[1, i]
        lses[i] = jnp.where(lane_n < HALF, a, pltpu.roll(b, HALF, 1))
        deltas[i] = jnp.where(lane_n < HALF, pltpu.roll(a, HALF, 1), b)
    for copy in copies:
        copy.wait()
    lane = lax.broadcasted_iota(jnp.int32, (HALF, 128), 1)
    sub = lax.broadcasted_iota(jnp.int32, (HALF, 128), 0) + c * HALF
    mine = lane == sub

    def step(s, carry):
        t = s * NX + x
        ok = sub < tab[32, t]
        where = []
        for k in range(NBR):
            u = tab[16 + k, t]
            ux, us = lax.rem(u, NX), lax.div(u, NX)
            tiles[k * BLK : k * BLK + HALF] = held[0, ux, us]
            tiles[k * BLK + HALF : (k + 1) * BLK] = held[1, ux, us]
            where.append((ux, us))
        lhs = split_rows(kv_ref[s])
        acc = jnp.zeros((BLK, 128), F32)
        for j in range(NBR // 2):
            both = lax.dot_general(lhs, tiles[j * 256 : j * 256 + 256], NT, preferred_element_type=F32)
            ps, ds = [], []
            for i in range(2):
                k = 2 * j + i
                ux, us = where[k]
                lse = lses[ux, pl.ds(us, 1), :]
                delta = deltas[ux, pl.ds(us, 1), :]
                p = jnp.exp2(both[:HALF, i * 128 : i * 128 + 128] * C2 - lse)
                p = jnp.where((ok | mine) if k == 0 else ok, p, 0.0)
                ps.append(p.astype(BF))
                ds.append((p * (both[HALF:, i * 128 : i * 128 + 128] - delta)).astype(BF))
            weights = jnp.concatenate([jnp.concatenate(ds, axis=1), jnp.concatenate(ps, axis=1)], axis=0)
            acc = acc + lax.dot_general(
                weights, tiles[j * 256 : j * 256 + 256], NN, preferred_element_type=F32
            )
        dkv_ref[s] = jnp.where(lane < HD, acc[:HALF] * SCALE, acc[HALF:]).astype(BF)
        return carry

    lax.fori_loop(0, NSRC, step, 0)


def ring(step):
    return [(i, (i + step) % NX) for i in range(NX)]


SWAP = [(0, 1), (1, 0)]


def gather_pieces(own):
    half = NSRC // 2
    r1 = lax.ppermute(own, "x", ring(1))
    l1 = lax.ppermute(own, "x", ring(-1))
    r2 = lax.ppermute(r1[:half], "x", ring(1))
    l2 = lax.ppermute(l1[half:], "x", ring(-1))
    pieces = (own, r1, l1, r2, l2)
    return pieces + tuple(lax.ppermute(a, "bend", SWAP) for a in pieces)


def per_device(queries, keys_in, values, d_out, token_count, block_ids, neighbours):
    c = lax.axis_index("bend")
    z = lax.axis_index("z")
    y = lax.axis_index("y")
    x = lax.axis_index("x")
    t_self = z * 16 + y * 4 + x
    limit = token_count[0] - lax.dynamic_index_in_dim(block_ids, t_self, 0, False) * BLK
    meta = jnp.stack([c, limit, x, c, c, c, c, c]).astype(jnp.int32)
    other_role = (z // 4) != c

    tile = (HEADS, HALF, 128)
    sent = pl.pallas_call(
        pack_other_kernel,
        out_shape=jax.ShapeDtypeStruct((2 * HEADS, HALF, 128), BF),
        in_specs=[SMEM] + [VMEM] * 4,
        out_specs=VMEM,
        compiler_params=PARAMS,
        cost_estimate=cost(0, 2**20),
        name="pack_other",
    )(meta, queries, keys_in, values, d_out)
    came = lax.ppermute(sent, "bend", SWAP)
    kv_out, qg_out = pl.pallas_call(
        pack_mine_kernel,
        out_shape=(jax.ShapeDtypeStruct((NSRC, HALF, 128), BF),) * 2,
        in_specs=[SMEM] + [VMEM] * 4,
        out_specs=(VMEM, VMEM),
        compiler_params=PARAMS,
        cost_estimate=cost(0, 2**20),
        name="pack_mine",
    )(meta, queries, keys_in, values, d_out)
    kv_out = lax.dynamic_update_slice_in_dim(kv_out, came[:HEADS], (1 - c) * HEADS, 0)
    qg_out = lax.dynamic_update_slice_in_dim(qg_out, came[HEADS:], (1 - c) * HEADS, 0)

    tab = make_tables(block_ids, neighbours, token_count)
    tab_other = lax.ppermute(tab, "bend", SWAP)
    tab = jnp.where(other_role, tab_other, tab)

    kv = lax.all_to_all(kv_out, ("z", "y"), 0, 0, tiled=True)
    qg = lax.all_to_all(qg_out, ("z", "y"), 0, 0, tiled=True)

    kv_pieces = gather_pieces(kv)
    qg_pieces = gather_pieces(qg)

    held = pltpu.VMEM((2, NX, NSRC, HALF, 128), BF)
    tiles = pltpu.VMEM((NBR * BLK, 128), BF)
    sems = pltpu.SemaphoreType.DMA((10,))
    dq, stat = pl.pallas_call(
        query_kernel,
        out_shape=(
            jax.ShapeDtypeStruct((NSRC, HALF // 2, 128), BF),
            jax.ShapeDtypeStruct((NSRC, 128), F32),
        ),
        in_specs=[SMEM, SMEM, VMEM] + [ANY] * 10,
        out_specs=(VMEM, VMEM),
        scratch_shapes=[held, tiles, pltpu.VMEM((2, NBR, HALF, 128), F32), sems],
        compiler_params=PARAMS,
        cost_estimate=cost(4 * 10**9, 5 * 2**20),
        name="query_side",
    )(meta, tab, qg, *kv_pieces)

    pair = lax.ppermute(stat, "bend", SWAP)
    stats = jnp.where(c == 0, jnp.stack([stat, pair]), jnp.stack([pair, stat]))
    shifted = [stats] + [lax.ppermute(stats, "x", ring(k)) for k in (1, 2, 3)]
    stats = jnp.stack([lax.select_n(lax.rem(x - i + NX, NX), *shifted) for i in range(NX)], axis=1)

    dkv = pl.pallas_call(
        key_kernel,
        out_shape=jax.ShapeDtypeStruct((NSRC, HALF, 128), BF),
        in_specs=[SMEM, SMEM, VMEM, VMEM] + [ANY] * 10,
        out_specs=VMEM,
        scratch_shapes=[
            held,
            tiles,
            pltpu.VMEM((NX, NSRC, 128), F32),
            pltpu.VMEM((NX, NSRC, 128), F32),
            sems,
        ],
        compiler_params=PARAMS,
        cost_estimate=cost(4 * 10**9, 5 * 2**20),
        name="key_side",
    )(meta, tab, kv, stats, *qg_pieces)

    dq_back = lax.all_to_all(dq, ("z", "y"), 0, 0, tiled=True)
    dq_other = lax.ppermute(
        lax.dynamic_slice_in_dim(dq_back, (1 - c) * HEADS, HEADS, 0), "bend", SWAP
    )
    grad_queries = pl.pallas_call(
        unpack_q_kernel,
        out_shape=jax.ShapeDtypeStruct(queries.shape, BF),
        in_specs=[SMEM, VMEM, VMEM],
        out_specs=VMEM,
        compiler_params=PARAMS,
        cost_estimate=cost(0, 2**19),
        name="unpack_q",
    )(meta, dq_back, dq_other)

    dkv_back = lax.all_to_all(dkv, ("z", "y"), 0, 0, tiled=True)
    dkv_other = lax.ppermute(
        lax.dynamic_slice_in_dim(dkv_back, (1 - c) * HEADS, HEADS, 0), "bend", SWAP
    )
    grad_keys, grad_values = pl.pallas_call(
        unpack_kv_kernel,
        out_shape=(jax.ShapeDtypeStruct(queries.shape, BF),) * 2,
        in_specs=[SMEM, VMEM, VMEM],
        out_specs=(VMEM, VMEM),
        compiler_params=PARAMS,
        cost_estimate=cost(0, 2**20),
        name="unpack_kv",
    )(meta, dkv_back, dkv_other)
    return grad_queries, grad_keys, grad_values


def solution(mesh):
    devices = mesh.devices.reshape(2, 8, 4, 4)
    fine = Mesh(devices, ("bend", "z", "y", "x"))
    rows = P(("bend", "z", "y", "x"), None)
    return jax.shard_map(
        per_device,
        mesh=fine,
        in_specs=(rows, rows, rows, rows, P("bend"), P("bend"), P("bend", None)),
        out_specs=(rows, rows, rows),
        check_vma=False,
    )
```

```python
import functools
import math

import jax
import jax.numpy as jnp
from jax import lax
from jax.experimental import pallas as pl
from jax.experimental.pallas import tpu as pltpu
from jax.sharding import Mesh, PartitionSpec as P

HD = 64
BLK = 128
HALF = 64
NBR = 10
HEADS = 16
NSRC = 32
NX = 4
UNROLL = 8
SCALE = 1.0 / math.sqrt(HD)
C2 = SCALE * math.log2(math.e)
NEG = -1e30
BF = jnp.bfloat16
F32 = jnp.float32
NT = (((1,), (1,)), ((), ()))
NN = (((1,), (0,)), ((), ()))
VMEM = pl.BlockSpec(memory_space=pltpu.VMEM)
SMEM = pl.BlockSpec(memory_space=pltpu.SMEM)
ANY = pl.BlockSpec(memory_space=pl.ANY)
HBM = pl.BlockSpec(memory_space=pltpu.HBM)
PARAMS = pltpu.CompilerParams(vmem_limit_bytes=60 * 2**20)
SMALL = pltpu.CompilerParams(vmem_limit_bytes=16 * 2**20)


def cost(flops, nbytes):
    return pl.CostEstimate(flops=flops, bytes_accessed=nbytes, transcendentals=0)


def tables_kernel(row_ref, col_ref, nbr_ref, nbrt_ref, out_ref):
    n = 128
    sub = lax.broadcasted_iota(jnp.int32, (n, n), 0)
    lane = lax.broadcasted_iota(jnp.int32, (n, n), 1)
    b_of = (col_ref[:, 0:1] == lane).astype(F32).astype(BF)
    adj = jnp.zeros((n, n), F32)
    adj_t = jnp.zeros((n, n), F32)
    for k in range(NBR):
        adj = adj + (nbr_ref[:, k : k + 1] == lane).astype(F32)
        adj_t = adj_t + (nbrt_ref[k : k + 1, :] == sub).astype(F32)
    eye = (sub == lane).astype(F32)
    tri = (lane <= sub).astype(F32).astype(BF)

    def stored(a):
        right = lax.dot_general(a.astype(BF), b_of, NT, preferred_element_type=F32)
        return lax.dot_general(b_of, right.astype(BF), NN, preferred_element_type=F32) - eye

    out_ref[...] = jnp.zeros_like(out_ref)
    own = lax.broadcasted_iota(jnp.int32, (1, n), 1)
    for base, a in ((0, adj_t), (16, adj)):
        m = stored(a)
        rank = lax.dot_general(tri, m.astype(BF), NN, preferred_element_type=F32)
        out_ref[base : base + 1, :] = own
        for k in range(1, NBR):
            hit = jnp.where((rank == float(k)) & (m > 0.5), sub, 0)
            out_ref[base + k : base + k + 1, :] = jnp.sum(hit, axis=0, keepdims=True)
    out_ref[32:33, :] = row_ref[1:2, :] - row_ref[0:1, :] * BLK


def make_tables(block_ids, neighbours, token_count):
    row = jnp.concatenate(
        [block_ids[None, :], jnp.broadcast_to(token_count[:1, None], (1, 128)), jnp.zeros((6, 128), jnp.int32)], 0
    )
    nbrt = jnp.concatenate([neighbours.T, jnp.full((6, 128), -1, jnp.int32)], 0)
    return pl.pallas_call(
        tables_kernel,
        out_shape=jax.ShapeDtypeStruct((40, 128), jnp.int32),
        in_specs=[VMEM] * 4,
        out_specs=VMEM,
        compiler_params=PARAMS,
        name="tables",
    )(row, block_ids[:, None], neighbours, nbrt)


def pack_half(half, ids, count, arrays, bufs, sems, kv_out, qg_out, base):
    row0 = pl.multiple_of(half * HALF, HALF)
    copies = [
        pltpu.make_async_copy(arrays[i].at[pl.ds(row0, HALF)], bufs.at[i], sems.at[i]) for i in (1, 2, 0, 3)
    ]
    for copy in copies:
        copy.start()
    t = lax.axis_index("z") * 16 + lax.axis_index("y") * 4 + lax.axis_index("x")
    limit = count[0] - ids[t] * BLK - row0
    keep = lax.broadcasted_iota(jnp.int32, (HALF, 128), 0) < limit
    for copy in copies:
        copy.wait()
    for p in range(HEADS // 2):
        cols = slice(p * 128, p * 128 + 128)
        q, k, v, g = (bufs[i, :, cols] for i in range(4))
        g = jnp.where(keep, g.astype(F32), 0.0).astype(BF)
        for out, m, n in ((kv_out, k, v), (qg_out, q, g)):
            out[base + 2 * p] = jnp.concatenate([m[:, :HD], n[:, :HD]], axis=1)
            out[base + 2 * p + 1] = jnp.concatenate([m[:, HD:], n[:, HD:]], axis=1)


def pack_other_kernel(ids, count, q_ref, k_ref, v_ref, g_ref, out_ref, bufs, sems):
    half = 1 - lax.axis_index("bend")
    kv_ref, qg_ref = out_ref.at[pl.ds(0, HEADS)], out_ref.at[pl.ds(HEADS, HEADS)]
    pack_half(half, ids, count, (q_ref, k_ref, v_ref, g_ref), bufs, sems, kv_ref, qg_ref, 0)


def pack_mine_kernel(ids, count, q_ref, k_ref, v_ref, g_ref, kv_ref, qg_ref, bufs, sems):
    half = lax.axis_index("bend")
    pack_half(half, ids, count, (q_ref, k_ref, v_ref, g_ref), bufs, sems, kv_ref, qg_ref, half * HEADS)


def unpack_kernel(full_ref, other_ref, q_ref, k_ref, v_ref):
    c = lax.axis_index("bend")
    h2 = HALF // 2
    for src, base, half in ((full_ref, c * HEADS, c), (other_ref, 0, 1 - c)):
        rows = pl.ds(pl.multiple_of(half * HALF, HALF), HALF)
        lo = pl.ds(pl.multiple_of(half * HALF, HALF), h2)
        hi = pl.ds(pl.multiple_of(half * HALF + h2, h2), h2)
        for p in range(HEADS // 2):
            cols = slice(p * 128, p * 128 + 128)
            a, b = src[base + 2 * p, :HALF], src[base + 2 * p + 1, :HALF]
            k_ref[rows, cols] = jnp.concatenate([a[:, :HD], b[:, :HD]], axis=1)
            v_ref[rows, cols] = jnp.concatenate([a[:, HD:], b[:, HD:]], axis=1)
            a, b = src[base + 2 * p, HALF:], src[base + 2 * p + 1, HALF:]
            q_ref[lo, cols] = jnp.concatenate([a[:, :HD], b[:, :HD]], axis=1)
            q_ref[hi, cols] = jnp.concatenate([a[:, HD:], b[:, HD:]], axis=1)


def fetch(pieces, dst, sems, c, x):
    half = NSRC // 2
    left, right, far = lax.rem(x + 3, NX), lax.rem(x + 1, NX), lax.rem(x + 2, NX)
    copies = []
    for side in range(2):
        o = c if side == 0 else 1 - c
        own, r1, l1, r2, l2 = pieces[5 * side : 5 * side + 5]
        for src, to in (
            (own, dst.at[o, x]),
            (r1, dst.at[o, left]),
            (l1, dst.at[o, right]),
            (r2, dst.at[o, far, pl.ds(0, half)]),
            (l2, dst.at[o, far, pl.ds(half, half)]),
        ):
            copies.append(pltpu.make_async_copy(src, to, sems.at[len(copies)]))
    return copies


def split_rows(tile):
    lane = lax.broadcasted_iota(jnp.int32, (HALF, 128), 1)
    low = (lane < HD).astype(F32).astype(BF)
    return jnp.concatenate([tile * low, tile * (1 - low)], axis=0)


def places(tab, base, t):
    out = []
    for k in range(NBR):
        u = tab[base + k, t]
        out.append((lax.rem(u, NX), lax.div(u, NX), u))
    return out


def load_pieces(pieces, held, sems):
    c, x = lax.axis_index("bend"), lax.axis_index("x")
    copies = fetch(pieces, held, sems, c, x)
    for copy in copies:
        copy.start()
    return c, x, copies


def gather_tiles(held, tiles, u, where):
    for k in range(NBR):
        for h in range(2):
            tiles[u, (2 * k + h) * HALF : (2 * k + h + 1) * HALF] = held[h, where[k][0], where[k][1]]


def skewed(stages):
    for r in range(UNROLL + len(stages) - 1):
        for n in range(len(stages)):
            if 0 <= r - n < UNROLL:
                stages[n](r - n)


def query_kernel(tab, qg_ref, *refs):
    pieces, (dq_ref, row_ref, held, tiles, scores, grads, sems) = refs[:10], refs[10:]
    c, x, copies = load_pieces(pieces, held, sems)
    for copy in copies:
        copy.wait()
    lane = lax.broadcasted_iota(jnp.int32, (HALF, 128), 1)
    sub = lax.broadcasted_iota(jnp.int32, (HALF, 128), 0)
    lane_row = lax.broadcasted_iota(jnp.int32, (1, 128), 1)
    mine = lane == sub + c * HALF

    def step(i, carry):
        ss = [i * UNROLL + u for u in range(UNROLL)]
        where = [places(tab, 0, s * NX + x) for s in ss]
        tops, totals = {}, {}

        def products(u):
            gather_tiles(held, tiles, u, where[u])
            lhs = split_rows(qg_ref[ss[u]])
            top = jnp.full((HALF, 128), NEG, F32)
            for j in range(NBR // 2):
                both = lax.dot_general(
                    lhs, tiles[u, j * 256 : j * 256 + 256], NT, preferred_element_type=F32
                )
                for i in range(2):
                    k = 2 * j + i
                    sc = both[:HALF, i * 128 : i * 128 + 128] * C2
                    limit = tab[32, where[u][k][2]]
                    if k == 0:
                        sc = jnp.where((lane < limit) | mine, sc, NEG)
                    else:
                        sc = sc + jnp.where(lane_row < limit, 0.0, NEG)
                    scores[u, 0, k] = sc
                    scores[u, 1, k] = both[HALF:, i * 128 : i * 128 + 128]
                    top = jnp.maximum(top, sc)
            tops[u] = jnp.max(top, axis=1, keepdims=True)

        def weights(u):
            total = jnp.zeros((HALF, 128), F32)
            dot = jnp.zeros((HALF, 128), F32)
            for k in range(NBR):
                p = jnp.exp2(scores[u, 0, k] - tops[u])
                scores[u, 0, k] = p
                total = total + p
                dot = dot + p * scores[u, 1, k]
            total = jnp.sum(total, axis=1, keepdims=True)
            totals[u] = total, jnp.sum(dot, axis=1, keepdims=True) / total

        def gradient(u):
            total, delta = totals[u]
            for k in range(NBR):
                grads[u, :, k * 128 : k * 128 + 128] = (scores[u, 0, k] * (scores[u, 1, k] - delta)).astype(BF)
            acc = lax.dot_general(grads[u], tiles[u], NN, preferred_element_type=F32)
            dq = (acc * (SCALE / total)).astype(BF)
            dq_ref[ss[u]] = jnp.concatenate([dq[: HALF // 2, :HD], dq[HALF // 2 :, :HD]], axis=1)
            lse = tops[u] + jnp.log2(total)
            row = jnp.where(lane == sub, lse, 0.0) + jnp.where(lane == sub + HALF, delta, 0.0)
            row = jnp.sum(row, axis=0, keepdims=True)
            for i in range(2 * NX):
                row_ref[i, pl.ds(ss[u], 1), :] = row

        skewed((products, weights, gradient))
        return carry

    lax.fori_loop(0, NSRC // UNROLL, step, 0)


def key_kernel(tab, kv_ref, dq_ref, stats_ref, *refs):
    pieces, (out_ref, held, tiles, scores, pairs, lses, deltas, sems) = refs[:10], refs[10:]
    c, x, copies = load_pieces(pieces, held, sems)
    lane_n = lax.broadcasted_iota(jnp.int32, (NSRC, 128), 1)
    for i in range(NX):
        a, b = stats_ref[i], stats_ref[NX + i]
        lse = jnp.where(lane_n < HALF, a, pltpu.roll(b, HALF, 1))
        delta = jnp.where(lane_n < HALF, pltpu.roll(a, HALF, 1), b)
        for s in range(NSRC):
            lses[i, s] = jnp.broadcast_to(lse[s : s + 1], (8, 128))
            deltas[i, s] = jnp.broadcast_to(delta[s : s + 1], (8, 128))
    out_ref[:, HALF:] = dq_ref[...]
    for copy in copies:
        copy.wait()
    lane = lax.broadcasted_iota(jnp.int32, (HALF, 128), 1)
    sub = lax.broadcasted_iota(jnp.int32, (HALF, 128), 0) + c * HALF
    mine = lane == sub

    def step(i, carry):
        ss = [i * UNROLL + u for u in range(UNROLL)]
        where = [places(tab, 16, s * NX + x) for s in ss]

        def products(u):
            gather_tiles(held, tiles, u, where[u])
            lhs = split_rows(kv_ref[ss[u]])
            for j in range(NBR // 2):
                both = lax.dot_general(
                    lhs, tiles[u, j * 256 : j * 256 + 256], NT, preferred_element_type=F32
                )
                for i in range(2):
                    k = 2 * j + i
                    scores[u, 0, k] = both[:HALF, i * 128 : i * 128 + 128]
                    scores[u, 1, k] = both[HALF:, i * 128 : i * 128 + 128]

        def weights(u):
            ok = sub < tab[32, ss[u] * NX + x]
            for k in range(NBR):
                ux, us, _ = where[u][k]
                lse = jnp.concatenate([lses[ux, us]] * 8, axis=0)
                delta = jnp.concatenate([deltas[ux, us]] * 8, axis=0)
                p = jnp.exp2(scores[u, 0, k] * C2 - lse)
                p = jnp.where((ok | mine) if k == 0 else ok, p, 0.0)
                pairs[u, :HALF, k * 128 : k * 128 + 128] = (p * (scores[u, 1, k] - delta)).astype(BF)
                pairs[u, HALF:, k * 128 : k * 128 + 128] = p.astype(BF)

        def gradient(u):
            acc = lax.dot_general(pairs[u], tiles[u], NN, preferred_element_type=F32)
            out_ref[ss[u], :HALF] = jnp.where(lane < HD, acc[:HALF] * SCALE, acc[HALF:]).astype(BF)

        skewed((products, weights, gradient))
        return carry

    lax.fori_loop(0, NSRC // UNROLL, step, 0)


def ring(step):
    return [(i, (i + step) % NX) for i in range(NX)]


SWAP = [(0, 1), (1, 0)]


def swap(a):
    return lax.ppermute(a, "bend", SWAP)


def first_step(own):
    return lax.ppermute(own, "x", ring(1)), lax.ppermute(own, "x", ring(-1))


def second_step(own, r1, l1):
    half = NSRC // 2
    r2 = lax.ppermute(r1[:half], "x", ring(1))
    l2 = lax.ppermute(l1[half:], "x", ring(-1))
    return own, r1, l1, r2, l2


def per_device(queries, keys_in, values, d_out, token_count, block_ids, neighbours):
    c = lax.axis_index("bend")
    other_role = (lax.axis_index("z") // 4) != c

    bufs = [pltpu.VMEM((4, HALF, HEADS * HD), BF), pltpu.SemaphoreType.DMA((4,))]
    sent = pl.pallas_call(
        pack_other_kernel,
        out_shape=jax.ShapeDtypeStruct((2 * HEADS, HALF, 128), BF),
        in_specs=[SMEM] * 2 + [HBM] * 4,
        out_specs=VMEM,
        scratch_shapes=bufs,
        compiler_params=PARAMS,
        cost_estimate=cost(0, 2**20),
        name="pack_other",
    )(block_ids, token_count, queries, keys_in, values, d_out)
    came = swap(sent)
    kv_out, qg_out = pl.pallas_call(
        pack_mine_kernel,
        out_shape=(jax.ShapeDtypeStruct((NSRC, HALF, 128), BF),) * 2,
        in_specs=[SMEM] * 2 + [HBM] * 4,
        out_specs=(VMEM, VMEM),
        scratch_shapes=bufs,
        compiler_params=PARAMS,
        cost_estimate=cost(0, 2**20),
        name="pack_mine",
    )(block_ids, token_count, queries, keys_in, values, d_out)
    theirs = (1 - c) * HEADS
    kv_out = lax.dynamic_update_slice_in_dim(kv_out, came[:HEADS], theirs, 0)
    qg_out = lax.dynamic_update_slice_in_dim(qg_out, came[HEADS:], theirs, 0)
    kv = lax.all_to_all(kv_out, ("z", "y"), 0, 0, tiled=True)
    kv, qg_out = lax.optimization_barrier((kv, qg_out))
    qg = lax.all_to_all(qg_out, ("z", "y"), 0, 0, tiled=True)

    tab = make_tables(block_ids, neighbours, token_count)
    tab = jnp.where(other_role, swap(tab), tab)

    r1, l1, tab = lax.optimization_barrier(first_step(kv) + (tab,))
    kv_pieces = second_step(kv, r1, l1)
    kv_pieces += tuple(swap(a) for a in kv_pieces)
    late = lax.optimization_barrier((qg,) + kv_pieces[3:5])
    qg_first = first_step(late[0])

    held = pltpu.VMEM((2, NX, NSRC, HALF, 128), BF)
    tiles = pltpu.VMEM((UNROLL, NBR * BLK, 128), BF)
    scores = pltpu.VMEM((UNROLL, 2, NBR, HALF, 128), F32)
    stat = pltpu.VMEM((NX, NSRC, 8, 128), F32)
    sems = pltpu.SemaphoreType.DMA((10,))
    dq, rows = pl.pallas_call(
        query_kernel,
        out_shape=(
            jax.ShapeDtypeStruct((NSRC, HALF // 2, 128), BF),
            jax.ShapeDtypeStruct((2 * NX, NSRC, 128), F32),
        ),
        in_specs=[SMEM, VMEM] + [ANY] * 10,
        out_specs=(VMEM, VMEM),
        scratch_shapes=[held, tiles, scores, pltpu.VMEM((UNROLL, HALF, NBR * BLK), BF), sems],
        compiler_params=PARAMS,
        cost_estimate=cost(6 * 10**9, 20 * 2**20),
        name="query_side",
    )(tab, qg, *kv_pieces)
    stats = lax.all_to_all(rows, ("bend", "x"), 0, 0, tiled=True)

    qg_first = lax.optimization_barrier(qg_first + (rows,))[:2]
    qg_pieces = second_step(qg, *qg_first)
    *qg_last, stats = lax.optimization_barrier(qg_pieces[3:] + (stats,))
    qg_pieces = qg_pieces[:3] + tuple(qg_last)
    qg_pieces += tuple(swap(a) for a in qg_pieces)

    grads = pl.pallas_call(
        key_kernel,
        out_shape=jax.ShapeDtypeStruct((NSRC, HALF + HALF // 2, 128), BF),
        in_specs=[SMEM, VMEM, VMEM, VMEM] + [ANY] * 10,
        out_specs=VMEM,
        scratch_shapes=[held, tiles, scores, pltpu.VMEM((UNROLL, BLK, NBR * BLK), BF), stat, stat, sems],
        compiler_params=PARAMS,
        cost_estimate=cost(6 * 10**9, 20 * 2**20),
        name="key_side",
    )(tab, kv, dq, stats, *qg_pieces)

    back = lax.all_to_all(grads, ("z", "y"), 0, 0, tiled=True)
    other = swap(lax.dynamic_slice_in_dim(back, theirs, HEADS, 0))
    return pl.pallas_call(
        unpack_kernel,
        out_shape=(jax.ShapeDtypeStruct(queries.shape, BF),) * 3,
        in_specs=[VMEM] * 2,
        out_specs=(VMEM, VMEM, VMEM),
        compiler_params=SMALL,
        cost_estimate=cost(0, 2**20),
        name="unpack",
    )(back, other)


def solution(mesh):
    devices = mesh.devices.reshape(2, 8, 4, 4)
    fine = Mesh(devices, ("bend", "z", "y", "x"))
    rows = P(("bend", "z", "y", "x"), None)
    return jax.shard_map(
        per_device,
        mesh=fine,
        in_specs=(rows, rows, rows, rows, P("bend"), P("bend"), P("bend", None)),
        out_specs=(rows, rows, rows),
        check_vma=False,
    )
```

```python
import functools
import math

import jax
import jax.numpy as jnp
from jax import lax
from jax.experimental import pallas as pl
from jax.experimental.pallas import tpu as pltpu
from jax.sharding import Mesh, PartitionSpec as P

HD = 64
BLK = 128
HALF = 64
NBR = 10
HEADS = 16
NSRC = 32
NX = 4
UNROLL = 16
SLOTS = 8
SCALE = 1.0 / math.sqrt(HD)
C2 = SCALE * math.log2(math.e)
NEG = -1e30
BF = jnp.bfloat16
F32 = jnp.float32
NT = (((1,), (1,)), ((), ()))
NN = (((1,), (0,)), ((), ()))
VMEM = pl.BlockSpec(memory_space=pltpu.VMEM)
SMEM = pl.BlockSpec(memory_space=pltpu.SMEM)
ANY = pl.BlockSpec(memory_space=pl.ANY)
HBM = pl.BlockSpec(memory_space=pltpu.HBM)
PARAMS = pltpu.CompilerParams(vmem_limit_bytes=60 * 2**20)
SMALL = pltpu.CompilerParams(vmem_limit_bytes=16 * 2**20)


def cost(flops, nbytes):
    return pl.CostEstimate(flops=flops, bytes_accessed=nbytes, transcendentals=0)


def tables_kernel(count, row_ref, nbrt_ref, out_ref):
    n = 128
    sub = lax.broadcasted_iota(jnp.int32, (n, n), 0)
    lane = lax.broadcasted_iota(jnp.int32, (n, n), 1)
    placed = (row_ref[...] == sub).astype(F32)
    adj_t = jnp.zeros((n, n), F32)
    for k in range(NBR):
        adj_t = adj_t + (nbrt_ref[k : k + 1, :] == sub).astype(F32)
    eye = (sub == lane).astype(F32)
    tri = (lane <= sub).astype(F32).astype(BF)
    right = lax.dot_general(adj_t.astype(BF), placed.astype(BF), NN, preferred_element_type=F32)
    near_t = lax.dot_general(placed.T.astype(BF), right.astype(BF), NN, preferred_element_type=F32) - eye
    out_ref[...] = jnp.zeros_like(out_ref)
    own = lax.broadcasted_iota(jnp.int32, (1, n), 1)
    for base, m in ((0, near_t), (16, near_t.T)):
        rank = lax.dot_general(tri, m.astype(BF), NN, preferred_element_type=F32)
        out_ref[base : base + 1, :] = own
        for k in range(1, NBR):
            hit = jnp.where((rank == float(k)) & (m > 0.5), sub, 0)
            out_ref[base + k : base + k + 1, :] = jnp.sum(hit, axis=0, keepdims=True)
    out_ref[32:33, :] = count[0] - row_ref[...] * BLK


def make_tables(block_ids, neighbours, token_count):
    return pl.pallas_call(
        tables_kernel,
        out_shape=jax.ShapeDtypeStruct((40, 128), jnp.int32),
        in_specs=[SMEM, VMEM, VMEM],
        out_specs=VMEM,
        compiler_params=SMALL,
        name="tables",
    )(token_count, block_ids[None, :], neighbours.T)


def pack_kernel(masked, ids, count, a_ref, b_ref, sent_ref, mine_ref, bufs, sems):
    copies = [pltpu.make_async_copy(src, bufs.at[i], sems.at[i]) for i, src in enumerate((a_ref, b_ref))]
    for copy in copies:
        copy.start()
    c = lax.axis_index("bend")
    t = lax.axis_index("z") * 16 + lax.axis_index("y") * 4 + lax.axis_index("x")
    limit = count[0] - ids[t] * BLK
    row = lax.broadcasted_iota(jnp.int32, (HALF, 128), 0)
    for copy in copies:
        copy.wait()
    for out, base, half in ((sent_ref, 0, 1 - c), (mine_ref, c * HEADS, c)):
        row0 = pl.multiple_of(half * HALF, HALF)
        for p in range(HEADS // 2):
            cols = slice(p * 128, p * 128 + 128)
            m, n = (bufs[i, pl.ds(row0, HALF), cols] for i in range(2))
            if masked:
                n = jnp.where(row + row0 < limit, n.astype(F32), 0.0).astype(BF)
            out[base + 2 * p] = jnp.concatenate([m[:, :HD], n[:, :HD]], axis=1)
            out[base + 2 * p + 1] = jnp.concatenate([m[:, HD:], n[:, HD:]], axis=1)


def pack(name, masked, ids, count, a, b):
    return pl.pallas_call(
        functools.partial(pack_kernel, masked),
        out_shape=(
            jax.ShapeDtypeStruct((HEADS, HALF, 128), BF),
            jax.ShapeDtypeStruct((NSRC, HALF, 128), BF),
        ),
        in_specs=[SMEM] * 2 + [HBM] * 2,
        out_specs=(VMEM, VMEM),
        scratch_shapes=[pltpu.VMEM((2, BLK, HEADS * HD), BF), pltpu.SemaphoreType.DMA((2,))],
        compiler_params=PARAMS,
        cost_estimate=cost(0, 2**20),
        name=name,
    )(ids, count, a, b)


def unpack_kernel(full_ref, other_ref, q_ref, k_ref, v_ref):
    c = lax.axis_index("bend")
    h2 = HALF // 2
    for src, base, half in ((full_ref, c * HEADS, c), (other_ref, 0, 1 - c)):
        rows = pl.ds(pl.multiple_of(half * HALF, HALF), HALF)
        lo = pl.ds(pl.multiple_of(half * HALF, HALF), h2)
        hi = pl.ds(pl.multiple_of(half * HALF + h2, h2), h2)
        for p in range(HEADS // 2):
            cols = slice(p * 128, p * 128 + 128)
            a, b = src[base + 2 * p, :HALF], src[base + 2 * p + 1, :HALF]
            k_ref[rows, cols] = jnp.concatenate([a[:, :HD], b[:, :HD]], axis=1)
            v_ref[rows, cols] = jnp.concatenate([a[:, HD:], b[:, HD:]], axis=1)
            a, b = src[base + 2 * p, HALF:], src[base + 2 * p + 1, HALF:]
            q_ref[lo, cols] = jnp.concatenate([a[:, :HD], b[:, :HD]], axis=1)
            q_ref[hi, cols] = jnp.concatenate([a[:, HD:], b[:, HD:]], axis=1)


def fetch(pieces, dst, sems, c, x):
    half = NSRC // 2
    left, right, far = lax.rem(x + 3, NX), lax.rem(x + 1, NX), lax.rem(x + 2, NX)
    copies = []
    for side in range(2):
        o = c if side == 0 else 1 - c
        own, r1, l1, r2, l2 = pieces[5 * side : 5 * side + 5]
        for src, to in (
            (own, dst.at[o, x]),
            (r1, dst.at[o, left]),
            (l1, dst.at[o, right]),
            (r2, dst.at[o, far, pl.ds(0, half)]),
            (l2, dst.at[o, far, pl.ds(half, half)]),
        ):
            copies.append(pltpu.make_async_copy(src, to, sems.at[len(copies)]))
    return copies


def split_rows(tile):
    lane = lax.broadcasted_iota(jnp.int32, (HALF, 128), 1)
    low = (lane < HD).astype(F32).astype(BF)
    return jnp.concatenate([tile * low, tile * (1 - low)], axis=0)


def places(tab, base, t):
    out = []
    for k in range(NBR):
        u = tab[base + k, t]
        out.append((lax.rem(u, NX), lax.div(u, NX), u))
    return out


def load_pieces(pieces, held, sems):
    c, x = lax.axis_index("bend"), lax.axis_index("x")
    copies = fetch(pieces, held, sems, c, x)
    for copy in copies:
        copy.start()
    return c, x, copies


def gather_tiles(held, tiles, u, where):
    for k in range(NBR):
        for h in range(2):
            tiles[u % SLOTS, (2 * k + h) * HALF : (2 * k + h + 1) * HALF] = held[h, where[k][0], where[k][1]]


def skewed(stages):
    for r in range(UNROLL + len(stages) - 1):
        for n in range(len(stages)):
            if 0 <= r - n < UNROLL:
                stages[n](r - n)


def query_kernel(tab, qg_ref, *refs):
    pieces, (dq_ref, row_ref, held, tiles, scores, grads, sems) = refs[:10], refs[10:]
    c, x, copies = load_pieces(pieces, held, sems)
    for copy in copies:
        copy.wait()
    lane = lax.broadcasted_iota(jnp.int32, (HALF, 128), 1)
    sub = lax.broadcasted_iota(jnp.int32, (HALF, 128), 0)
    lane_row = lax.broadcasted_iota(jnp.int32, (1, 128), 1)
    mine = lane == sub + c * HALF

    def step(i, carry):
        ss = [i * UNROLL + u for u in range(UNROLL)]
        where = [places(tab, 0, s * NX + x) for s in ss]
        tops, totals = {}, {}

        def products(u):
            gather_tiles(held, tiles, u, where[u])
            lhs = split_rows(qg_ref[ss[u]])
            top = jnp.full((HALF, 128), NEG, F32)
            for j in range(NBR // 2):
                both = lax.dot_general(
                    lhs, tiles[u % SLOTS, j * 256 : j * 256 + 256], NT, preferred_element_type=F32
                )
                for i in range(2):
                    k = 2 * j + i
                    sc = both[:HALF, i * 128 : i * 128 + 128] * C2
                    limit = tab[32, where[u][k][2]]
                    if k == 0:
                        sc = jnp.where((lane < limit) | mine, sc, NEG)
                    else:
                        sc = sc + jnp.where(lane_row < limit, 0.0, NEG)
                    scores[u % SLOTS, 0, k] = sc
                    scores[u % SLOTS, 1, k] = both[HALF:, i * 128 : i * 128 + 128]
                    top = jnp.maximum(top, sc)
            tops[u] = jnp.max(top, axis=1, keepdims=True)

        def weights(u):
            total = jnp.zeros((HALF, 128), F32)
            dot = jnp.zeros((HALF, 128), F32)
            for k in range(NBR):
                p = jnp.exp2(scores[u % SLOTS, 0, k] - tops[u])
                scores[u % SLOTS, 0, k] = p
                total = total + p
                dot = dot + p * scores[u % SLOTS, 1, k]
            total = jnp.sum(total, axis=1, keepdims=True)
            totals[u] = total, jnp.sum(dot, axis=1, keepdims=True) / total

        def gradient(u):
            total, delta = totals[u]
            for k in range(NBR):
                grads[u % SLOTS, :, k * 128 : k * 128 + 128] = (scores[u % SLOTS, 0, k] * (scores[u % SLOTS, 1, k] - delta)).astype(BF)
            acc = lax.dot_general(grads[u % SLOTS], tiles[u % SLOTS], NN, preferred_element_type=F32)
            dq = (acc * (SCALE / total)).astype(BF)
            dq_ref[ss[u]] = jnp.concatenate([dq[: HALF // 2, :HD], dq[HALF // 2 :, :HD]], axis=1)
            lse = tops[u] + jnp.log2(total)
            row = jnp.where(lane == sub, lse, 0.0) + jnp.where(lane == sub + HALF, delta, 0.0)
            row = jnp.sum(row, axis=0, keepdims=True)
            for i in range(2 * NX):
                row_ref[i, pl.ds(ss[u], 1), :] = row

        skewed((products, weights, gradient))
        return carry

    lax.fori_loop(0, NSRC // UNROLL, step, 0)


def key_kernel(tab, kv_ref, dq_ref, stats_ref, *refs):
    pieces, (out_ref, held, tiles, scores, pairs, lses, deltas, sems) = refs[:10], refs[10:]
    c, x, copies = load_pieces(pieces, held, sems)
    lane_n = lax.broadcasted_iota(jnp.int32, (NSRC, 128), 1)
    for i in range(NX):
        a, b = stats_ref[i], stats_ref[NX + i]
        lse = jnp.where(lane_n < HALF, a, pltpu.roll(b, HALF, 1))
        delta = jnp.where(lane_n < HALF, pltpu.roll(a, HALF, 1), b)
        for s in range(NSRC):
            lses[i, s] = jnp.broadcast_to(lse[s : s + 1], (8, 128))
            deltas[i, s] = jnp.broadcast_to(delta[s : s + 1], (8, 128))
    out_ref[:, HALF:] = dq_ref[...]
    for copy in copies:
        copy.wait()
    lane = lax.broadcasted_iota(jnp.int32, (HALF, 128), 1)
    sub = lax.broadcasted_iota(jnp.int32, (HALF, 128), 0) + c * HALF
    mine = lane == sub

    def step(i, carry):
        ss = [i * UNROLL + u for u in range(UNROLL)]
        where = [places(tab, 16, s * NX + x) for s in ss]

        def products(u):
            gather_tiles(held, tiles, u, where[u])
            lhs = split_rows(kv_ref[ss[u]])
            for j in range(NBR // 2):
                both = lax.dot_general(
                    lhs, tiles[u % SLOTS, j * 256 : j * 256 + 256], NT, preferred_element_type=F32
                )
                for i in range(2):
                    k = 2 * j + i
                    scores[u % SLOTS, 0, k] = both[:HALF, i * 128 : i * 128 + 128]
                    scores[u % SLOTS, 1, k] = both[HALF:, i * 128 : i * 128 + 128]

        def weights(u):
            ok = sub < tab[32, ss[u] * NX + x]
            for k in range(NBR):
                ux, us, _ = where[u][k]
                lse = jnp.concatenate([lses[ux, us]] * 8, axis=0)
                delta = jnp.concatenate([deltas[ux, us]] * 8, axis=0)
                p = jnp.exp2(scores[u % SLOTS, 0, k] * C2 - lse)
                p = jnp.where((ok | mine) if k == 0 else ok, p, 0.0)
                pairs[u % SLOTS, :HALF, k * 128 : k * 128 + 128] = (p * (scores[u % SLOTS, 1, k] - delta)).astype(BF)
                pairs[u % SLOTS, HALF:, k * 128 : k * 128 + 128] = p.astype(BF)

        def gradient(u):
            acc = lax.dot_general(pairs[u % SLOTS], tiles[u % SLOTS], NN, preferred_element_type=F32)
            out_ref[ss[u], :HALF] = jnp.where(lane < HD, acc[:HALF] * SCALE, acc[HALF:]).astype(BF)

        skewed((products, weights, gradient))
        return carry

    lax.fori_loop(0, NSRC // UNROLL, step, 0)


def ring(step):
    return [(i, (i + step) % NX) for i in range(NX)]


SWAP = [(0, 1), (1, 0)]


def swap(a):
    return lax.ppermute(a, "bend", SWAP)


def first_step(own):
    return lax.ppermute(own, "x", ring(1)), lax.ppermute(own, "x", ring(-1))


def second_step(own, r1, l1):
    half = NSRC // 2
    r2 = lax.ppermute(r1[:half], "x", ring(1))
    l2 = lax.ppermute(l1[half:], "x", ring(-1))
    return own, r1, l1, r2, l2


def per_device(queries, keys_in, values, d_out, token_count, block_ids, neighbours):
    c = lax.axis_index("bend")
    other_role = (lax.axis_index("z") // 4) != c

    theirs = (1 - c) * HEADS
    kv_sent, kv_mine = pack("pack_kv", False, block_ids, token_count, keys_in, values)
    kv_came = swap(kv_sent)
    qg_sent, qg_mine = pack("pack_qg", True, block_ids, token_count, queries, d_out)
    kv_out = lax.dynamic_update_slice_in_dim(kv_mine, kv_came, theirs, 0)
    kv_out, qg_sent, qg_mine = lax.optimization_barrier((kv_out, qg_sent, qg_mine))
    kv = lax.all_to_all(kv_out, ("z", "y"), 0, 0, tiled=True)
    kv, qg_sent = lax.optimization_barrier((kv, qg_sent))
    qg_out = lax.dynamic_update_slice_in_dim(qg_mine, swap(qg_sent), theirs, 0)
    qg = lax.all_to_all(qg_out, ("z", "y"), 0, 0, tiled=True)

    tab = make_tables(block_ids, neighbours, token_count)
    tab = jnp.where(other_role, swap(tab), tab)

    r1, l1, tab = lax.optimization_barrier(first_step(kv) + (tab,))
    kv_pieces = second_step(kv, r1, l1)
    kv_pieces += tuple(swap(a) for a in kv_pieces)
    late = lax.optimization_barrier((qg,) + kv_pieces[3:5])
    qg_first = first_step(late[0])

    held = pltpu.VMEM((2, NX, NSRC, HALF, 128), BF)
    tiles = pltpu.VMEM((SLOTS, NBR * BLK, 128), BF)
    scores = pltpu.VMEM((SLOTS, 2, NBR, HALF, 128), F32)
    stat = pltpu.VMEM((NX, NSRC, 8, 128), F32)
    sems = pltpu.SemaphoreType.DMA((10,))
    dq, rows = pl.pallas_call(
        query_kernel,
        out_shape=(
            jax.ShapeDtypeStruct((NSRC, HALF // 2, 128), BF),
            jax.ShapeDtypeStruct((2 * NX, NSRC, 128), F32),
        ),
        in_specs=[SMEM, VMEM] + [ANY] * 10,
        out_specs=(VMEM, VMEM),
        scratch_shapes=[held, tiles, scores, pltpu.VMEM((SLOTS, HALF, NBR * BLK), BF), sems],
        compiler_params=PARAMS,
        cost_estimate=cost(6 * 10**9, 20 * 2**20),
        name="query_side",
    )(tab, qg, *kv_pieces)
    stats = lax.all_to_all(rows, ("bend", "x"), 0, 0, tiled=True)

    qg_first = lax.optimization_barrier(qg_first + (rows,))[:2]
    qg_pieces = second_step(qg, *qg_first)
    *qg_last, stats = lax.optimization_barrier(qg_pieces[3:] + (stats,))
    qg_pieces = qg_pieces[:3] + tuple(qg_last)
    qg_pieces += tuple(swap(a) for a in qg_pieces)

    grads = pl.pallas_call(
        key_kernel,
        out_shape=jax.ShapeDtypeStruct((NSRC, HALF + HALF // 2, 128), BF),
        in_specs=[SMEM, VMEM, VMEM, VMEM] + [ANY] * 10,
        out_specs=VMEM,
        scratch_shapes=[held, tiles, scores, pltpu.VMEM((SLOTS, BLK, NBR * BLK), BF), stat, stat, sems],
        compiler_params=PARAMS,
        cost_estimate=cost(6 * 10**9, 20 * 2**20),
        name="key_side",
    )(tab, kv, dq, stats, *qg_pieces)

    back = lax.all_to_all(grads, ("z", "y"), 0, 0, tiled=True)
    other = swap(lax.dynamic_slice_in_dim(back, theirs, HEADS, 0))
    return pl.pallas_call(
        unpack_kernel,
        out_shape=(jax.ShapeDtypeStruct(queries.shape, BF),) * 3,
        in_specs=[VMEM] * 2,
        out_specs=(VMEM, VMEM, VMEM),
        compiler_params=SMALL,
        cost_estimate=cost(0, 2**20),
        name="unpack",
    )(back, other)


def solution(mesh):
    devices = mesh.devices.reshape(2, 8, 4, 4)
    fine = Mesh(devices, ("bend", "z", "y", "x"))
    rows = P(("bend", "z", "y", "x"), None)
    return jax.shard_map(
        per_device,
        mesh=fine,
        in_specs=(rows, rows, rows, rows, P("bend"), P("bend"), P("bend", None)),
        out_specs=(rows, rows, rows),
        check_vma=False,
    )
```

```python
import functools
import math

import jax
import jax.numpy as jnp
from jax import lax
from jax.experimental import pallas as pl
from jax.experimental.pallas import tpu as pltpu
from jax.sharding import Mesh, PartitionSpec as P

HD = 64
BLK = 128
HALF = 64
NBR = 10
HEADS = 16
NSRC = 32
NX = 4
UNROLL = 16
SLOTS = 8
SCALE = 1.0 / math.sqrt(HD)
C2 = SCALE * math.log2(math.e)
NEG = -1e30
BF = jnp.bfloat16
F32 = jnp.float32
NT = (((1,), (1,)), ((), ()))
NN = (((1,), (0,)), ((), ()))
VMEM = pl.BlockSpec(memory_space=pltpu.VMEM)
SMEM = pl.BlockSpec(memory_space=pltpu.SMEM)
ANY = pl.BlockSpec(memory_space=pl.ANY)
HBM = pl.BlockSpec(memory_space=pltpu.HBM)
PARAMS = pltpu.CompilerParams(vmem_limit_bytes=60 * 2**20)
SMALL = pltpu.CompilerParams(vmem_limit_bytes=16 * 2**20)


def cost(flops, nbytes):
    return pl.CostEstimate(flops=flops, bytes_accessed=nbytes, transcendentals=0)


def tables_kernel(count, row_ref, nbrt_ref, out_ref):
    n = 128
    sub = lax.broadcasted_iota(jnp.int32, (n, n), 0)
    lane = lax.broadcasted_iota(jnp.int32, (n, n), 1)
    placed = (row_ref[...] == sub).astype(F32)
    adj_t = jnp.zeros((n, n), F32)
    for k in range(NBR):
        adj_t = adj_t + (nbrt_ref[k : k + 1, :] == sub).astype(F32)
    eye = (sub == lane).astype(F32)
    tri = (lane <= sub).astype(F32).astype(BF)
    right = lax.dot_general(adj_t.astype(BF), placed.astype(BF), NN, preferred_element_type=F32)
    near_t = lax.dot_general(placed.T.astype(BF), right.astype(BF), NN, preferred_element_type=F32) - eye
    out_ref[...] = jnp.zeros_like(out_ref)
    own = lax.broadcasted_iota(jnp.int32, (1, n), 1)
    for base, m in ((0, near_t), (16, near_t.T)):
        rank = lax.dot_general(tri, m.astype(BF), NN, preferred_element_type=F32)
        out_ref[base : base + 1, :] = own
        for k in range(1, NBR):
            hit = jnp.where((rank == float(k)) & (m > 0.5), sub, 0)
            out_ref[base + k : base + k + 1, :] = jnp.sum(hit, axis=0, keepdims=True)
    out_ref[32:33, :] = count[0] - row_ref[...] * BLK


def make_tables(block_ids, neighbours, token_count):
    return pl.pallas_call(
        tables_kernel,
        out_shape=jax.ShapeDtypeStruct((40, 128), jnp.int32),
        in_specs=[SMEM, VMEM, VMEM],
        out_specs=VMEM,
        compiler_params=SMALL,
        name="tables",
    )(token_count, block_ids[None, :], neighbours.T)


def pack_kernel(masked, ids, count, a_ref, b_ref, sent_ref, mine_ref, bufs, sems):
    copies = [pltpu.make_async_copy(src, bufs.at[i], sems.at[i]) for i, src in enumerate((a_ref, b_ref))]
    for copy in copies:
        copy.start()
    c = lax.axis_index("bend")
    t = lax.axis_index("z") * 16 + lax.axis_index("y") * 4 + lax.axis_index("x")
    limit = count[0] - ids[t] * BLK
    row = lax.broadcasted_iota(jnp.int32, (HALF, 128), 0)
    for copy in copies:
        copy.wait()
    for out, base, half in ((sent_ref, 0, 1 - c), (mine_ref, c * HEADS, c)):
        row0 = pl.multiple_of(half * HALF, HALF)
        for p in range(HEADS // 2):
            cols = slice(p * 128, p * 128 + 128)
            m, n = (bufs[i, pl.ds(row0, HALF), cols] for i in range(2))
            if masked:
                n = jnp.where(row + row0 < limit, n.astype(F32), 0.0).astype(BF)
            out[base + 2 * p] = jnp.concatenate([m[:, :HD], n[:, :HD]], axis=1)
            out[base + 2 * p + 1] = jnp.concatenate([m[:, HD:], n[:, HD:]], axis=1)


def pack(name, masked, ids, count, a, b):
    return pl.pallas_call(
        functools.partial(pack_kernel, masked),
        out_shape=(
            jax.ShapeDtypeStruct((HEADS, HALF, 128), BF),
            jax.ShapeDtypeStruct((NSRC, HALF, 128), BF),
        ),
        in_specs=[SMEM] * 2 + [HBM] * 2,
        out_specs=(VMEM, VMEM),
        scratch_shapes=[pltpu.VMEM((2, BLK, HEADS * HD), BF), pltpu.SemaphoreType.DMA((2,))],
        compiler_params=PARAMS,
        cost_estimate=cost(0, 2**20),
        name=name,
    )(ids, count, a, b)


def unpack_kernel(full_ref, other_ref, q_ref, k_ref, v_ref):
    c = lax.axis_index("bend")
    h2 = HALF // 2
    for src, base, half in ((full_ref, c * HEADS, c), (other_ref, 0, 1 - c)):
        rows = pl.ds(pl.multiple_of(half * HALF, HALF), HALF)
        lo = pl.ds(pl.multiple_of(half * HALF, HALF), h2)
        hi = pl.ds(pl.multiple_of(half * HALF + h2, h2), h2)
        for p in range(HEADS // 2):
            cols = slice(p * 128, p * 128 + 128)
            a, b = src[base + 2 * p, :HALF], src[base + 2 * p + 1, :HALF]
            k_ref[rows, cols] = jnp.concatenate([a[:, :HD], b[:, :HD]], axis=1)
            v_ref[rows, cols] = jnp.concatenate([a[:, HD:], b[:, HD:]], axis=1)
            a, b = src[base + 2 * p, HALF:], src[base + 2 * p + 1, HALF:]
            q_ref[lo, cols] = jnp.concatenate([a[:, :HD], b[:, :HD]], axis=1)
            q_ref[hi, cols] = jnp.concatenate([a[:, HD:], b[:, HD:]], axis=1)


def fetch(pieces, dst, sems, c, x):
    half = NSRC // 2
    left, right, far = lax.rem(x + 3, NX), lax.rem(x + 1, NX), lax.rem(x + 2, NX)
    copies = []
    for side in range(2):
        o = c if side == 0 else 1 - c
        own, r1, l1, r2, l2 = pieces[5 * side : 5 * side + 5]
        for src, to in (
            (own, dst.at[o, x]),
            (r1, dst.at[o, left]),
            (l1, dst.at[o, right]),
            (r2, dst.at[o, far, pl.ds(0, half)]),
            (l2, dst.at[o, far, pl.ds(half, half)]),
        ):
            copies.append(pltpu.make_async_copy(src, to, sems.at[len(copies)]))
    return copies


def split_rows(tile):
    lane = lax.broadcasted_iota(jnp.int32, (HALF, 128), 1)
    low = (lane < HD).astype(F32).astype(BF)
    return jnp.concatenate([tile * low, tile * (1 - low)], axis=0)


def places(tab, base, t):
    out = []
    for k in range(NBR):
        u = tab[base + k, t]
        out.append((lax.rem(u, NX), lax.div(u, NX), u))
    return out


def load_pieces(pieces, held, sems):
    c, x = lax.axis_index("bend"), lax.axis_index("x")
    copies = fetch(pieces, held, sems, c, x)
    for copy in copies:
        copy.start()
    return c, x, copies


def gather_tiles(held, tiles, u, where):
    for k in range(NBR):
        for h in range(2):
            tiles[u % SLOTS, (2 * k + h) * HALF : (2 * k + h + 1) * HALF] = held[h, where[k][0], where[k][1]]


def skewed(stages):
    for r in range(UNROLL + len(stages) - 1):
        for n in range(len(stages)):
            if 0 <= r - n < UNROLL:
                stages[n](r - n)


def query_kernel(tab, qg_ref, *refs):
    pieces, (dq_ref, row_ref, held, tiles, scores, grads, sems) = refs[:10], refs[10:]
    c, x, copies = load_pieces(pieces, held, sems)
    for copy in copies:
        copy.wait()
    lane = lax.broadcasted_iota(jnp.int32, (HALF, 128), 1)
    sub = lax.broadcasted_iota(jnp.int32, (HALF, 128), 0)
    lane_row = lax.broadcasted_iota(jnp.int32, (1, 128), 1)
    mine = lane == sub + c * HALF

    def step(i, carry):
        ss = [i * UNROLL + u for u in range(UNROLL)]
        where = [places(tab, 0, s * NX + x) for s in ss]
        tops, totals = {}, {}

        def products(u):
            gather_tiles(held, tiles, u, where[u])
            lhs = split_rows(qg_ref[ss[u]])
            top = jnp.full((HALF, 128), NEG, F32)
            for j in range(NBR // 2):
                both = lax.dot_general(
                    lhs, tiles[u % SLOTS, j * 256 : j * 256 + 256], NT, preferred_element_type=F32
                )
                for i in range(2):
                    k = 2 * j + i
                    sc = both[:HALF, i * 128 : i * 128 + 128] * C2
                    limit = tab[32, where[u][k][2]]
                    if k == 0:
                        sc = jnp.where((lane < limit) | mine, sc, NEG)
                    else:
                        sc = sc + jnp.where(lane_row < limit, 0.0, NEG)
                    scores[u % SLOTS, 0, k] = sc
                    scores[u % SLOTS, 1, k] = both[HALF:, i * 128 : i * 128 + 128]
                    top = jnp.maximum(top, sc)
            tops[u] = jnp.max(top, axis=1, keepdims=True)

        def weights(u):
            total = jnp.zeros((HALF, 128), F32)
            dot = jnp.zeros((HALF, 128), F32)
            for k in range(NBR):
                p = jnp.exp2(scores[u % SLOTS, 0, k] - tops[u])
                scores[u % SLOTS, 0, k] = p
                total = total + p
                dot = dot + p * scores[u % SLOTS, 1, k]
            total = jnp.sum(total, axis=1, keepdims=True)
            totals[u] = total, jnp.sum(dot, axis=1, keepdims=True) / total

        def gradient(u):
            total, delta = totals[u]
            for k in range(NBR):
                grads[u % SLOTS, :, k * 128 : k * 128 + 128] = (scores[u % SLOTS, 0, k] * (scores[u % SLOTS, 1, k] - delta)).astype(BF)
            acc = lax.dot_general(grads[u % SLOTS], tiles[u % SLOTS], NN, preferred_element_type=F32)
            dq = (acc * (SCALE / total)).astype(BF)
            dq_ref[ss[u]] = jnp.concatenate([dq[: HALF // 2, :HD], dq[HALF // 2 :, :HD]], axis=1)
            lse = tops[u] + jnp.log2(total)
            row = jnp.where(lane == sub, lse, 0.0) + jnp.where(lane == sub + HALF, delta, 0.0)
            row_ref[pl.ds(ss[u], 1), :] = jnp.sum(row, axis=0, keepdims=True)

        skewed((products, weights, gradient))
        return carry

    lax.fori_loop(0, NSRC // UNROLL, step, 0)


def key_kernel(tab, kv_ref, dq_ref, stats_ref, *refs):
    pieces, (out_ref, held, tiles, scores, pairs, lses, deltas, sems) = refs[:10], refs[10:]
    c, x, copies = load_pieces(pieces, held, sems)
    lane_n = lax.broadcasted_iota(jnp.int32, (NSRC, 128), 1)
    for i in range(NX):
        a, b = stats_ref[i, c], stats_ref[i, 1 - c]
        lse = jnp.where(lane_n < HALF, a, pltpu.roll(b, HALF, 1))
        delta = jnp.where(lane_n < HALF, pltpu.roll(a, HALF, 1), b)
        for s in range(NSRC):
            lses[i, s] = jnp.broadcast_to(lse[s : s + 1], (8, 128))
            deltas[i, s] = jnp.broadcast_to(delta[s : s + 1], (8, 128))
    out_ref[:, HALF:] = dq_ref[...]
    for copy in copies:
        copy.wait()
    lane = lax.broadcasted_iota(jnp.int32, (HALF, 128), 1)
    sub = lax.broadcasted_iota(jnp.int32, (HALF, 128), 0) + c * HALF
    mine = lane == sub

    def step(i, carry):
        ss = [i * UNROLL + u for u in range(UNROLL)]
        where = [places(tab, 16, s * NX + x) for s in ss]

        def products(u):
            gather_tiles(held, tiles, u, where[u])
            lhs = split_rows(kv_ref[ss[u]])
            for j in range(NBR // 2):
                both = lax.dot_general(
                    lhs, tiles[u % SLOTS, j * 256 : j * 256 + 256], NT, preferred_element_type=F32
                )
                for i in range(2):
                    k = 2 * j + i
                    scores[u % SLOTS, 0, k] = both[:HALF, i * 128 : i * 128 + 128]
                    scores[u % SLOTS, 1, k] = both[HALF:, i * 128 : i * 128 + 128]

        def weights(u):
            ok = sub < tab[32, ss[u] * NX + x]
            for k in range(NBR):
                ux, us, _ = where[u][k]
                lse = jnp.concatenate([lses[ux, us]] * 8, axis=0)
                delta = jnp.concatenate([deltas[ux, us]] * 8, axis=0)
                p = jnp.exp2(scores[u % SLOTS, 0, k] * C2 - lse)
                p = jnp.where((ok | mine) if k == 0 else ok, p, 0.0)
                pairs[u % SLOTS, :HALF, k * 128 : k * 128 + 128] = (p * (scores[u % SLOTS, 1, k] - delta)).astype(BF)
                pairs[u % SLOTS, HALF:, k * 128 : k * 128 + 128] = p.astype(BF)

        def gradient(u):
            acc = lax.dot_general(pairs[u % SLOTS], tiles[u % SLOTS], NN, preferred_element_type=F32)
            out_ref[ss[u], :HALF] = jnp.where(lane < HD, acc[:HALF] * SCALE, acc[HALF:]).astype(BF)

        skewed((products, weights, gradient))
        return carry

    lax.fori_loop(0, NSRC // UNROLL, step, 0)


def ring(step):
    return [(i, (i + step) % NX) for i in range(NX)]


SWAP = [(0, 1), (1, 0)]


def swap(a):
    return lax.ppermute(a, "bend", SWAP)


def first_step(own):
    return lax.ppermute(own, "x", ring(1)), lax.ppermute(own, "x", ring(-1))


def second_step(own, r1, l1):
    half = NSRC // 2
    r2 = lax.ppermute(r1[:half], "x", ring(1))
    l2 = lax.ppermute(l1[half:], "x", ring(-1))
    return own, r1, l1, r2, l2


def per_device(queries, keys_in, values, d_out, token_count, block_ids, neighbours):
    c = lax.axis_index("bend")
    other_role = (lax.axis_index("z") // 4) != c

    theirs = (1 - c) * HEADS
    kv_sent, kv_mine = pack("pack_kv", False, block_ids, token_count, keys_in, values)
    kv_came = swap(kv_sent)
    qg_sent, qg_mine = pack("pack_qg", True, block_ids, token_count, queries, d_out)
    kv_out = lax.dynamic_update_slice_in_dim(kv_mine, kv_came, theirs, 0)
    kv_out, qg_sent, qg_mine = lax.optimization_barrier((kv_out, qg_sent, qg_mine))
    kv = lax.all_to_all(kv_out, ("z", "y"), 0, 0, tiled=True)
    kv, qg_sent = lax.optimization_barrier((kv, qg_sent))
    qg_out = lax.dynamic_update_slice_in_dim(qg_mine, swap(qg_sent), theirs, 0)
    qg = lax.all_to_all(qg_out, ("z", "y"), 0, 0, tiled=True)

    tab = make_tables(block_ids, neighbours, token_count)
    tab = jnp.where(other_role, swap(tab), tab)

    r1, l1, tab = lax.optimization_barrier(first_step(kv) + (tab,))
    kv_pieces = second_step(kv, r1, l1)
    kv_pieces += tuple(swap(a) for a in kv_pieces)
    late = lax.optimization_barrier((qg,) + kv_pieces[3:5])
    qg_first = first_step(late[0])

    held = pltpu.VMEM((2, NX, NSRC, HALF, 128), BF)
    tiles = pltpu.VMEM((SLOTS, NBR * BLK, 128), BF)
    scores = pltpu.VMEM((SLOTS, 2, NBR, HALF, 128), F32)
    stat = pltpu.VMEM((NX, NSRC, 8, 128), F32)
    sems = pltpu.SemaphoreType.DMA((10,))
    dq, rows = pl.pallas_call(
        query_kernel,
        out_shape=(
            jax.ShapeDtypeStruct((NSRC, HALF // 2, 128), BF),
            jax.ShapeDtypeStruct((NSRC, 128), F32),
        ),
        in_specs=[SMEM, VMEM] + [ANY] * 10,
        out_specs=(VMEM, VMEM),
        scratch_shapes=[held, tiles, scores, pltpu.VMEM((SLOTS, HALF, NBR * BLK), BF), sems],
        compiler_params=PARAMS,
        cost_estimate=cost(6 * 10**9, 20 * 2**20),
        name="query_side",
    )(tab, qg, *kv_pieces)
    both = jnp.stack([rows, swap(rows)])
    stats = lax.all_to_all(jnp.broadcast_to(both, (NX,) + both.shape), "x", 0, 0, tiled=True)

    qg_first = lax.optimization_barrier(qg_first + (rows,))[:2]
    qg_pieces = second_step(qg, *qg_first)
    *qg_last, stats = lax.optimization_barrier(qg_pieces[3:] + (stats,))
    qg_pieces = qg_pieces[:3] + tuple(qg_last)
    qg_pieces += tuple(swap(a) for a in qg_pieces)

    grads = pl.pallas_call(
        key_kernel,
        out_shape=jax.ShapeDtypeStruct((NSRC, HALF + HALF // 2, 128), BF),
        in_specs=[SMEM, VMEM, VMEM, VMEM] + [ANY] * 10,
        out_specs=VMEM,
        scratch_shapes=[held, tiles, scores, pltpu.VMEM((SLOTS, BLK, NBR * BLK), BF), stat, stat, sems],
        compiler_params=PARAMS,
        cost_estimate=cost(6 * 10**9, 20 * 2**20),
        name="key_side",
    )(tab, kv, dq, stats, *qg_pieces)

    back = lax.all_to_all(grads, ("z", "y"), 0, 0, tiled=True)
    other = swap(lax.dynamic_slice_in_dim(back, theirs, HEADS, 0))
    return pl.pallas_call(
        unpack_kernel,
        out_shape=(jax.ShapeDtypeStruct(queries.shape, BF),) * 3,
        in_specs=[VMEM] * 2,
        out_specs=(VMEM, VMEM, VMEM),
        compiler_params=SMALL,
        cost_estimate=cost(0, 2**20),
        name="unpack",
    )(back, other)


def solution(mesh):
    devices = mesh.devices.reshape(2, 8, 4, 4)
    fine = Mesh(devices, ("bend", "z", "y", "x"))
    rows = P(("bend", "z", "y", "x"), None)
    return jax.shard_map(
        per_device,
        mesh=fine,
        in_specs=(rows, rows, rows, rows, P("bend"), P("bend"), P("bend", None)),
        out_specs=(rows, rows, rows),
        check_vma=False,
    )
```
